32 devices in a mesh: groups: 2 (over x), pool: 16 (over z, y, core).
Axes of the slice: x: 2, y: 2, z: 4, core: 2. Of those that a mesh axis runs over, the one named last changes fastest.
Arguments:
- query_embed: bfloat16 [256, 1024], P(('groups', 'pool')), parts along dimension 0, may hold values from -40 to 40
- key_slab: bfloat16 [8192, 1024], P(('groups', 'pool')), parts along dimension 0, may hold values from -4 to 4
- nbr_owner: int32 [256, 2], P(('groups', 'pool')), parts along dimension 0, may hold values from 0 to 15, all different within a row; in each aligned block of 8 rows (0 to 7, 8 to 15, ...) at most 2 rows name the same one
- nbr_slot: int32 [256, 2], P(('groups', 'pool')), parts along dimension 0, may hold values from 0 to 3
- enc_table: bfloat16 [128, 64, 896], P(('groups', 'pool')), parts along dimension 0, may hold values from -6 to 6
- stretch_queries: bfloat16 [16384, 2048], P(('groups', 'pool')), parts along dimension 0, may hold values from -6 to 6
- kv_weight: bfloat16 [896, 4096], P(None, 'pool'), may hold values from -0.1875 to 0.1875
Outputs:
- retrieval_lse: float32 [256], P(('groups', 'pool')), parts along dimension 0
- cross_mix: bfloat16 [16384, 2048], P(('groups', 'pool')), parts along dimension 0
The draws below stay inside these ranges and needn't reach their ends.
There are 2 independent parts, one for each index of `groups`. The reference program is written for one: setup_inputs(seed, part) draws one part's arguments, and reference() takes and returns one part's arrays. A program takes and returns all parts, laid end to end along the dimension named above; an argument that names none is the same for every part. Nothing has to cross between parts.
Inputs may be any that keep to these rules, and one draw needn't show every extreme that they name: `nbr_owner`: each row names two different owners. Among the rows of one device no owner is named more than 2 times, and in every draw some device names some owner exactly 2 times.
All inputs are finite; a program needn't handle non-finite values.
Results may differ from the reference program's by a relative error of at most 0.0072.
Values may be sent and summed in bfloat16 or wider, within the bound.
A program may use at most 128 MiB of HBM per device.

```python
import math
import jax
import jax.numpy as jnp
import numpy as np
from jax import lax

E = 1024
ENC = 896
HEADS = 16
HD = 128
CTOK = 64
NTOK = 64
CAP = 2
Q_DEV = 8
ENC_DEV = 4
QUERIES = 128
KEYS = 4096
ENC_ALL = 64
TOKENS = 8192
N_POOL = 16


def retrieval_pair(key):
    base = jax.random.fold_in(key, 7)
    key_first, key_second, key_third = jax.random.split(base, 3)
    keys_all = jnp.clip(jax.random.normal(key_first, (KEYS, E), jnp.float32), -4.0, 4.0)
    queries = jnp.clip(jax.random.normal(key_second, (QUERIES, E), jnp.float32), -4.0, 4.0)
    picks = jnp.arange(8, dtype=jnp.int32)
    key_index = picks * (KEYS // 8)
    query_index = picks * (QUERIES // 8)
    signs = jnp.where(jax.random.normal(key_third, (8, E), jnp.float32) > 0.0, 1.0, -1.0)
    target = (100.0 + 60.0 * (picks % 4)).astype(jnp.float32)
    keys_all = keys_all.at[key_index].set(4.0 * signs)
    keys_all = keys_all.at[key_index + 1].set(4.0 * signs * (1.0 - 2.0 / target)[:, None])
    factor = target / (4.0 * E ** 0.5)
    queries = queries.at[query_index].set(factor[:, None] * signs)
    return (queries, keys_all)


def draw_query_embed(key, part):
    return retrieval_pair(key)[0].astype(jnp.bfloat16)


def draw_key_slab(key, part):
    return retrieval_pair(key)[1].astype(jnp.bfloat16)


def with_ends(values, rng, least, high):
    longest = values.shape.index(max(values.shape))
    spots = []
    for shift in (0, 1):
        where = [jax.random.randint(jax.random.fold_in(rng, axis), (), 0, length) for axis, length in enumerate(values.shape)]
        where[longest] = (where[longest] + shift) % values.shape[longest]
        spots.append(tuple(where))
    return values.at[spots[0]].set(least).at[spots[1]].set(high)


def shard_levels(own_key, dims, shards, low, largest):
    gain = 1.0
    for position, parts in shards:
        heights = jax.random.uniform(jax.random.fold_in(jax.random.fold_in(own_key, 6), position), (parts,), jnp.float32, low / len(shards), largest / len(shards))
        gain = gain * jnp.repeat(jnp.exp(heights), dims[position] // parts).reshape((-1,) + (1,) * (len(dims) - 1 - position))
    return gain


def shared_out(key, own, number, rows, count, top, reach, slope):
    ranking = jax.random.permutation(key, count)
    heavy_load, usual = load_shares(count, rows * top, reach, slope, True), load_shares(count, rows * top, reach, slope, False)
    places = jnp.arange(count)

    def named(tallies, rotation):
        used = int((tallies > 0).sum())
        fixed = max(1, used // 4)
        passed = fixed + (places - fixed + rotation * (used - fixed)) % max(1, count - fixed)
        return jnp.zeros((count,), jnp.int32).at[ranking[jnp.where(places < fixed, places, passed)]].set(jnp.asarray(tallies, jnp.int32))

    tallies = jnp.where(number % 4 == 0, named(heavy_load, number // 4), named(usual, number - number // 4 - 1))
    mixed = jax.random.permutation(jax.random.fold_in(own, 3), count)
    giver, taker = mixed[0:count // 2 * 2:2], mixed[1:count // 2 * 2:2]
    slack = jnp.minimum(tallies[giver] - 1, reach - tallies[taker]) // 2
    slack = jnp.where((giver == ranking[0]) | (taker == ranking[0]) | (tallies[taker] == 0), 0, jnp.maximum(slack, 0))
    passed = jax.random.randint(jax.random.fold_in(own, 4), (count // 2,), 0, 1 << 20) % (slack + 1)
    tallies = tallies.at[giver].add(-passed).at[taker].add(passed)
    members = jnp.searchsorted(jnp.cumsum(tallies), jnp.arange(rows * top), side="right").astype(jnp.int32)
    table = members.reshape(top, rows).T
    table = table[jax.random.permutation(jax.random.fold_in(own, 1), rows)]
    rotation = jax.random.randint(jax.random.fold_in(own, 2), (rows, 1), 0, top)
    return jnp.take_along_axis(table, (jnp.arange(top)[None, :] + rotation) % top, axis=1)


def load_shares(amount, total, most, skew, full):
    weights = [(1 << 20) // math.isqrt(grade ** skew) + 1 for grade in range(1, amount + 1)]
    largest = most if full else min(most, max(-(-total // amount), total * weights[0] // sum(weights)))
    least = 1 if total - largest >= amount - 1 else 0
    holding, rest = [largest] + [least] * (amount - 1), total - largest - least * (amount - 1)
    while rest > 0:
        candidates = [i for i in range(1, amount) if holding[i] < largest] or [i for i in range(1, amount) if holding[i] < most]
        mass, budget = sum([weights[i] for i in candidates]), rest
        for i in candidates:
            extra = min(most - holding[i], max(1, budget * weights[i] // mass), rest)
            holding[i] = holding[i] + extra
            rest = rest - extra
    return np.array(holding)


def normal_values(own_key, shape, deviation, limit, cuts=(), held_as=jnp.bfloat16):
    values = jax.random.normal(own_key, shape, jnp.float32) * deviation
    if len(cuts) > 0:
        values = shard_levels(own_key, shape, cuts, -0.22, 0.18) * values
    return jnp.clip(values, min=-limit, max=limit).astype(held_as)


def setup_inputs(seed: int = 0, part: int = 0) -> dict:
    keys = jax.random.split(jax.random.key(seed), 8)
    part_splits = jax.random.split(jax.random.fold_in(keys[7], part), 8)
    query_embed = draw_query_embed(jax.random.fold_in(jax.random.fold_in(keys[7], part), 71), part)
    key_slab = draw_key_slab(jax.random.fold_in(jax.random.fold_in(keys[7], part), 71), part)
    nbr_owner_keys = jax.random.split(jax.random.fold_in(part_splits[2], 1), QUERIES // Q_DEV)
    nbr_owner_turns = jax.random.permutation(jax.random.fold_in(part_splits[2], 3), QUERIES // Q_DEV)
    nbr_owner = jax.vmap(lambda own, number: shared_out(jax.random.fold_in(part_splits[2], 2), own, number, Q_DEV, N_POOL, 2, CAP, 2))(nbr_owner_keys, nbr_owner_turns).reshape((QUERIES, 2))
    nbr_slot = with_ends(jax.random.randint(part_splits[3], (QUERIES, 2), 0, ENC_DEV), jax.random.fold_in(part_splits[3], 1), 0, ENC_DEV - 1).astype(jnp.int32)
    enc_table = normal_values(part_splits[4], (ENC_ALL, NTOK, ENC), 1.0, 6.0, ((0, 16),))
    stretch_queries = normal_values(part_splits[5], (TOKENS, HEADS * HD), 1.0, 6.0, ((0, 16),))
    kv_weight = normal_values(keys[6], (ENC, 2 * HEADS * HD), ENC ** -0.5, 0.1875, ((1, 16),))
    return {"query_embed": query_embed, "key_slab": key_slab, "nbr_owner": nbr_owner, "nbr_slot": nbr_slot, "enc_table": enc_table, "stretch_queries": stretch_queries, "kv_weight": kv_weight}


def reference(query_embed, key_slab, nbr_owner, nbr_slot, enc_table, stretch_queries, kv_weight):
    raw_scores = jnp.dot(query_embed, key_slab.T, preferred_element_type=jnp.float32) * (E ** -0.5)
    top_score = jnp.max(raw_scores, axis=1, keepdims=True)
    retrieval_lse = top_score[:, 0] + jnp.log(jnp.sum(jnp.exp(raw_scores - top_score), axis=1))

    def project(entry):
        return jnp.dot(entry, kv_weight, preferred_element_type=jnp.float32).astype(jnp.bfloat16)

    kv_table = lax.map(project, enc_table)
    width = HEADS * HD
    neighbour_ids = (nbr_owner * ENC_DEV + nbr_slot).astype(jnp.int32)
    grouped_queries = stretch_queries.reshape(QUERIES, CTOK, HEADS, HD)

    def attend(inputs):
        stretch_rows, stretch_ids = inputs
        picked = jnp.take(kv_table, stretch_ids, axis=0).reshape(2 * NTOK, 2 * width)
        key_part = picked[:, :width].reshape(2 * NTOK, HEADS, HD).astype(jnp.float32)
        value_part = picked[:, width:].reshape(2 * NTOK, HEADS, HD).astype(jnp.float32)
        logits = jnp.einsum("qhd,khd->hqk", stretch_rows.astype(jnp.float32), key_part) * (HD ** -0.5)
        expo = jnp.exp(logits)
        probs = (expo / jnp.sum(expo, axis=-1, keepdims=True)).astype(jnp.bfloat16)
        mixed = jnp.einsum("hqk,khd->qhd", probs.astype(jnp.float32), value_part)
        return mixed.astype(jnp.bfloat16).reshape(CTOK, width)

    cross_mix = lax.map(attend, (grouped_queries, neighbour_ids)).reshape(TOKENS, width)
    return retrieval_lse, cross_mix
```

```python
import functools

import jax
import jax.numpy as jnp
from jax import lax
from jax.experimental import pallas as pl
from jax.experimental.pallas import tpu as pltpu
from jax.sharding import PartitionSpec as P

HEADS = 16
MESH = pl.DeviceIdType.MESH
F32 = jnp.float32
BF16 = jnp.bfloat16
NT = (((1,), (1,)), ((), ()))


def attention(queries, keys, values, scale):
    logits = lax.dot_general(queries, keys, NT, preferred_element_type=F32) * scale
    expo = jnp.exp(logits)
    probs = (expo / jnp.sum(expo, axis=-1, keepdims=True)).astype(BF16)
    return jnp.dot(probs, values, preferred_element_type=F32).astype(BF16)


def kernel(
    owner_ref, slot_ref, embed_ref, key_ref, enc_ref, queries_ref, weight_ref,
    lse_ref, mix_ref,
    enc_all, weight_all, embed_own, embed_all, part_out, part_all, rows, queries_own, pair_kv,
    send_sem, local_sem, enc_sem, embed_sem, weight_sem, part_sem,
):
    pool = lax.axis_size("pool")
    x = lax.axis_index("groups")
    me = lax.axis_index("pool")
    z, y, c = me // 4, (me // 2) % 2, me % 2
    table = enc_ref.shape[0]
    quarter = weight_ref.shape[0] // 4
    sites = iter(range(send_sem.shape[0]))
    sends = []
    inner = (z + 1) // 2 == 1

    def at(zz, yy, cc):
        return (zz * 2 + yy) * 2 + cc

    side_y, side_c = at(z, 1 - y, c), at(z, y, 1 - c)
    near, mid = at(z + 1 - 2 * (z % 2), y, c), at(3 - z, y, c)
    z_from = (z + 1 - 2 * (z % 2), 2 - z // 2, 3 - 3 * (z // 2))
    z_to = (at(3 - z, y, c), at(3 * z - 3, y, c), at(3 * z - 3, y, c))
    X = {"groups": 1 - x, "pool": me}

    def to(pool_index):
        return {"groups": x, "pool": pool_index}

    def enc_piece(p):
        return enc_all.at[pl.ds(p * table, table)], enc_sem.at[p]

    def embed_piece(p):
        return embed_all.at[p], embed_sem.at[p]

    def weight_piece(number, p):
        start = pl.multiple_of(number * quarter, quarter)
        return weight_all.at[p, pl.ds(start, quarter)], weight_sem.at[p * 4 + number]

    def send(piece, target, when=None, source=None):
        ref, sem = piece
        index = next(sites)
        copy = pltpu.make_async_remote_copy(
            src_ref=ref if source is None else source, dst_ref=ref, send_sem=send_sem.at[index],
            recv_sem=sem, device_id=target, device_id_type=MESH)
        sends.append((copy, when))
        if when is None:
            copy.start()
        else:
            pl.when(when)(copy.start)

    def arrived(piece):
        ref, sem = piece
        pltpu.make_async_remote_copy(
            src_ref=ref, dst_ref=ref, send_sem=send_sem.at[0], recv_sem=sem, device_id=to(side_c),
            device_id_type=MESH).wait_recv()

    barrier = pltpu.get_barrier_semaphore()
    for step in range(1, pool):
        pl.semaphore_signal(barrier, inc=1, device_id=to((me + step) % pool), device_id_type=MESH)
    pl.semaphore_signal(barrier, inc=1, device_id=X, device_id_type=MESH)

    enc_local = pltpu.make_async_copy(enc_ref, enc_piece(me)[0], local_sem.at[0])
    enc_local.start()
    weight_local = pltpu.make_async_copy(weight_ref, weight_all.at[me], local_sem.at[1])
    weight_local.start()
    queries_local = pltpu.make_async_copy(queries_ref, queries_own, local_sem.at[2])
    queries_local.start()
    embed = embed_ref[...].astype(F32)
    half = embed.shape[1] // 2
    folded = jnp.concatenate([embed[:, :half], embed[:, half:]], axis=0).astype(BF16)
    embed_own[...] = folded
    embed_all[me] = folded
    pl.semaphore_wait(barrier, pool)

    own_a, own_b = x * 2, x * 2 + 1
    other_a, other_b = 2 - x * 2, 3 - x * 2

    def own_weight(number):
        return weight_ref.at[pl.ds(pl.multiple_of(number * quarter, quarter), quarter)]

    b_piece, a_piece = weight_piece(own_b, me), weight_piece(own_a, me)
    send(enc_piece(me), to(near), source=enc_ref)
    send(enc_piece(me), to(mid), inner, source=enc_ref)
    send(b_piece, to(side_y), source=own_weight(own_b))
    send(enc_piece(me), to(side_y), source=enc_ref)
    send(embed_piece(me), to(near), source=embed_own)
    send(embed_piece(me), to(mid), inner, source=embed_own)
    send(embed_piece(me), to(side_y), source=embed_own)
    send(embed_piece(me), to(side_c), source=embed_own)
    send(enc_piece(me), to(side_c), source=enc_ref)
    send(b_piece, to(near), source=own_weight(own_b))
    send(b_piece, to(mid), inner, source=own_weight(own_b))
    send(a_piece, to(near), source=own_weight(own_a))
    send(a_piece, to(mid), inner, source=own_weight(own_a))
    send(a_piece, to(side_y), source=own_weight(own_a))
    for number in range(4):
        send(weight_piece(number, me), to(side_c), source=own_weight(number))

    piece = weight_piece(own_b, side_y)
    arrived(piece)
    send(piece, to(near))
    send(piece, to(mid), inner)
    send(piece, X)
    send(piece, to(side_c))

    def from_y(zz):
        p = at(zz, 1 - y, c)
        arrived(embed_piece(p))
        send(embed_piece(p), to(side_c))
        arrived(enc_piece(p))
        send(enc_piece(p), to(side_c))
        piece = weight_piece(own_a, p)
        arrived(piece)
        send(piece, X)
        send(piece, to(side_c))

    for step in range(3):
        p = at(z_from[step], y, c)
        for piece in (embed_piece(p), enc_piece(p)):
            arrived(piece)
            send(piece, to(z_to[step]), inner)
            send(piece, to(side_y))
            send(piece, to(side_c))
        for yy in (y, 1 - y):
            piece = weight_piece(own_b, at(z_from[step], yy, c))
            arrived(piece)
            send(piece, to(z_to[step]), inner)
            send(piece, X)
            send(piece, to(side_c))
        piece = weight_piece(own_a, p)
        arrived(piece)
        send(piece, to(z_to[step]), inner)
        send(piece, to(side_y))
        send(piece, X)
        send(piece, to(side_c))
        from_y(z if step == 0 else z_from[step - 1])
    from_y(z_from[2])

    for zz in range(4):
        for yy in range(2):
            arrived(embed_piece(at(zz, yy, 1 - c)))
    embeds = embed_all[...].reshape(-1, half)
    first = lax.dot_general(embeds, key_ref[:, :half], NT, preferred_element_type=F32)
    second = lax.dot_general(embeds, key_ref[:, half:], NT, preferred_element_type=F32)
    count = embed.shape[0]
    keys = first.shape[1]
    first = first.reshape(pool, 2 * count, keys)[:, :count]
    second = second.reshape(pool, 2 * count, keys)[:, count:]
    scores = (first + second).reshape(pool * count, keys) * (2 * half) ** (-0.5)
    top = jnp.max(scores, axis=1, keepdims=True)
    part = top + jnp.log(jnp.sum(jnp.exp(scores - top), axis=1, keepdims=True))
    part_out[...] = jnp.broadcast_to(part, (pool * count, 128)).reshape(pool, count, 128)
    part_all[me] = part_out[me]
    for step in range(1, pool):
        d = (me + step) % pool
        copy = pltpu.make_async_remote_copy(
            src_ref=part_out.at[d], dst_ref=part_all.at[me], send_sem=send_sem.at[next(sites)],
            recv_sem=part_sem.at[me], device_id=to(d), device_id_type=MESH)
        copy.start()
        sends.append((copy, None))

    piece = weight_piece(other_b, side_y)
    arrived(piece)
    send(piece, to(side_c))
    for step in range(3):
        for number, yy in ((other_b, y), (other_b, 1 - y), (other_a, y)):
            piece = weight_piece(number, at(z_from[step], yy, c))
            arrived(piece)
            send(piece, to(side_c))
        piece = weight_piece(other_a, at(z if step == 0 else z_from[step - 1], 1 - y, c))
        arrived(piece)
        send(piece, to(side_c))
    piece = weight_piece(other_a, at(z_from[2], 1 - y, c))
    arrived(piece)
    send(piece, to(side_c))

    enc_local.wait()
    weight_local.wait()
    queries_local.wait()
    for zz in range(4):
        for yy in range(2):
            p = at(zz, yy, 1 - c)
            arrived(enc_piece(p))
            for number in range(4):
                arrived(weight_piece(number, p))

    tokens = enc_ref.shape[1]
    picks = owner_ref.shape[1]
    for i in range(count):
        for t in range(picks):
            row = (i * picks + t) * tokens
            rows[row:row + tokens, :] = enc_all[owner_ref[i, t] * table + slot_ref[i, t]]

    width = weight_ref.shape[1]
    head_dim = queries_ref.shape[1] // HEADS
    span = picks * tokens
    stretch = queries_ref.shape[0] // count
    scale = head_dim ** (-0.5)

    def pair(step, carry):
        lane = pl.multiple_of(step * width, width)
        pair_kv[0] = jnp.dot(rows[...], weight_all[step], preferred_element_type=F32).astype(BF16)
        pair_kv[1] = jnp.dot(
            rows[...], weight_all[step + pool // 2], preferred_element_type=F32).astype(BF16)
        for i in range(count):
            q = queries_own[i * stretch:(i + 1) * stretch, pl.ds(lane, width)]
            k = pair_kv[0, i * span:(i + 1) * span]
            v = pair_kv[1, i * span:(i + 1) * span]
            mixed = [
                attention(q[:, h:h + head_dim], k[:, h:h + head_dim], v[:, h:h + head_dim], scale)
                for h in range(0, width, head_dim)
            ]
            mix_ref[i * stretch:(i + 1) * stretch, pl.ds(lane, width)] = jnp.concatenate(mixed, axis=1)
        return carry

    lax.fori_loop(0, pool // 2, pair, 0)

    for step in range(1, pool):
        p = (me + step) % pool
        pltpu.make_async_remote_copy(
            src_ref=part_out.at[0], dst_ref=part_all.at[p], send_sem=send_sem.at[0],
            recv_sem=part_sem.at[p], device_id=to(side_c), device_id_type=MESH).wait_recv()
    parts = part_all[...]
    largest = jnp.max(parts, axis=0)
    lse_ref[...] = largest + jnp.log(jnp.sum(jnp.exp(parts - largest[None]), axis=0))
    for copy, when in sends:
        if when is None:
            copy.wait_send()
        else:
            pl.when(when)(copy.wait_send)


def kernel_local(query_embed, key_slab, nbr_owner, nbr_slot, enc_table, stretch_queries, kv_weight):
    pool = lax.axis_size("pool")
    count, wide = query_embed.shape
    vmem = pl.BlockSpec(memory_space=pltpu.VMEM)
    smem = pl.BlockSpec(memory_space=pltpu.SMEM)
    any_space = pl.BlockSpec(memory_space=pl.ANY)
    dma = pltpu.SemaphoreType.DMA
    found = count * nbr_owner.shape[1] * enc_table.shape[1]
    lse, mix = pl.pallas_call(
        kernel,
        out_shape=(
            jax.ShapeDtypeStruct((count, 128), F32),
            jax.ShapeDtypeStruct(stretch_queries.shape, BF16),
        ),
        in_specs=[smem, smem, vmem, vmem, any_space, any_space, any_space],
        out_specs=(vmem, vmem),
        scratch_shapes=[
            pltpu.VMEM((pool * enc_table.shape[0],) + enc_table.shape[1:], BF16),
            pltpu.VMEM((pool,) + kv_weight.shape, BF16),
            pltpu.VMEM((2 * count, wide // 2), BF16),
            pltpu.VMEM((pool, 2 * count, wide // 2), BF16),
            pltpu.VMEM((pool, count, 128), F32),
            pltpu.VMEM((pool, count, 128), F32),
            pltpu.VMEM((found, enc_table.shape[2]), BF16),
            pltpu.VMEM(stretch_queries.shape, BF16),
            pltpu.VMEM((2, found, kv_weight.shape[1]), BF16),
            dma((130,)),
            dma((3,)),
            dma((pool,)),
            dma((pool,)),
            dma((pool * 4,)),
            dma((pool,)),
        ],
        compiler_params=pltpu.CompilerParams(
            collective_id=0, has_side_effects=True, vmem_limit_bytes=48 * 1024 * 1024),
    )(nbr_owner, nbr_slot, query_embed, key_slab, enc_table, stretch_queries, kv_weight)
    return lse[:, 0], mix


def gathered_local(query_embed, key_slab, nbr_owner, nbr_slot, enc_table, stretch_queries, kv_weight):
    me = lax.axis_index("pool")
    count = query_embed.shape[0]
    scores = lax.dot_general(
        lax.all_gather(query_embed, "pool", axis=0, tiled=True), key_slab, NT,
        preferred_element_type=F32) * query_embed.shape[1] ** (-0.5)
    top = jnp.max(scores, axis=1, keepdims=True)
    part = top[:, 0] + jnp.log(jnp.sum(jnp.exp(scores - top), axis=1))
    parts = lax.dynamic_slice_in_dim(lax.all_gather(part, "pool"), me * count, count, 1)
    largest = jnp.max(parts, axis=0)
    lse = largest + jnp.log(jnp.sum(jnp.exp(parts - largest), axis=0))
    table = lax.all_gather(enc_table, "pool", axis=0, tiled=True)
    wanted = (nbr_owner * enc_table.shape[0] + nbr_slot).reshape(-1)
    rows = jnp.take(table, wanted, axis=0).reshape(-1, enc_table.shape[2])
    projected = jnp.dot(
        rows, lax.all_gather(kv_weight, "pool", axis=1, tiled=True),
        preferred_element_type=F32).astype(BF16)
    width = stretch_queries.shape[1]
    head_dim = width // HEADS
    key_part = projected[:, :width].reshape(count, -1, HEADS, head_dim)
    value_part = projected[:, width:].reshape(count, -1, HEADS, head_dim)
    grouped = stretch_queries.reshape(count, -1, HEADS, head_dim)
    logits = jnp.einsum(
        "cqhd,ckhd->chqk", grouped, key_part, preferred_element_type=F32) * head_dim ** (-0.5)
    expo = jnp.exp(logits)
    probs = (expo / jnp.sum(expo, axis=-1, keepdims=True)).astype(BF16)
    mixed = jnp.einsum("chqk,ckhd->cqhd", probs, value_part, preferred_element_type=F32)
    return lse, mixed.astype(BF16).reshape(-1, width)


def solution(mesh):
    in_specs = (
        P(("groups", "pool"), None),
        P(("groups", "pool"), None),
        P(("groups", "pool"), None),
        P(("groups", "pool"), None),
        P(("groups", "pool"), None, None),
        P(("groups", "pool"), None),
        P(None, "pool"),
    )
    out_specs = (P(("groups", "pool")), P(("groups", "pool"), None))
    routed = mesh.shape["groups"] == 2 and mesh.shape["pool"] == 16
    return jax.shard_map(
        kernel_local if routed else gathered_local, mesh=mesh, in_specs=in_specs, out_specs=out_specs,
        check_vma=False)
```

```python
import functools

import jax
import jax.numpy as jnp
from jax import lax
from jax.experimental import pallas as pl
from jax.experimental.pallas import tpu as pltpu
from jax.sharding import PartitionSpec as P

HEADS = 16
MESH = pl.DeviceIdType.MESH
F32 = jnp.float32
BF16 = jnp.bfloat16
NT = (((1,), (1,)), ((), ()))


def kernel(
    owner_ref, slot_ref, embed_ref, key_hbm, enc_ref, queries_ref, weight_ref,
    lse_ref, mix_ref,
    enc_all, weight_all, embed_own, embed_all, part_out, part_all, rows, queries_own, pair_kv, key_ref,
    send_sem, local_sem, enc_sem, embed_sem, weight_sem, part_sem,
):
    pool = lax.axis_size("pool")
    x = lax.axis_index("groups")
    me = lax.axis_index("pool")
    z, y, c = me // 4, (me // 2) % 2, me % 2
    table = enc_ref.shape[0]
    quarter = weight_ref.shape[0] // 4
    sites = iter(range(send_sem.shape[0]))
    sends = []
    inner = (z + 1) // 2 == 1

    def at(zz, yy, cc):
        return (zz * 2 + yy) * 2 + cc

    side_y, side_c = at(z, 1 - y, c), at(z, y, 1 - c)
    near, mid = at(z + 1 - 2 * (z % 2), y, c), at(3 - z, y, c)
    z_from = (z + 1 - 2 * (z % 2), 2 - z // 2, 3 - 3 * (z // 2))
    z_to = (at(3 - z, y, c), at(3 * z - 3, y, c), at(3 * z - 3, y, c))
    X = {"groups": 1 - x, "pool": me}

    def to(pool_index):
        return {"groups": x, "pool": pool_index}

    def enc_piece(p):
        return enc_all.at[pl.ds(p * table, table)], enc_sem.at[p]

    def embed_piece(p):
        return embed_all.at[p], embed_sem.at[p]

    def weight_piece(number, p):
        start = pl.multiple_of(number * quarter, quarter)
        return weight_all.at[p, pl.ds(start, quarter)], weight_sem.at[p * 4 + number]

    def send(piece, target, when=None, source=None):
        ref, sem = piece
        index = next(sites)
        copy = pltpu.make_async_remote_copy(
            src_ref=ref if source is None else source, dst_ref=ref, send_sem=send_sem.at[index],
            recv_sem=sem, device_id=target, device_id_type=MESH)
        sends.append((copy, when))
        if when is None:
            copy.start()
        else:
            pl.when(when)(copy.start)

    def arrived(piece):
        ref, sem = piece
        pltpu.make_async_remote_copy(
            src_ref=ref, dst_ref=ref, send_sem=send_sem.at[0], recv_sem=sem, device_id=to(side_c),
            device_id_type=MESH).wait_recv()

    barrier = pltpu.get_barrier_semaphore()
    for step in range(1, pool):
        pl.semaphore_signal(barrier, inc=1, device_id=to((me + step) % pool), device_id_type=MESH)
    pl.semaphore_signal(barrier, inc=1, device_id=X, device_id_type=MESH)

    enc_local = pltpu.make_async_copy(enc_ref, enc_piece(me)[0], local_sem.at[0])
    enc_local.start()
    weight_local = pltpu.make_async_copy(weight_ref, weight_all.at[me], local_sem.at[1])
    weight_local.start()
    queries_local = pltpu.make_async_copy(queries_ref, queries_own, local_sem.at[2])
    queries_local.start()
    key_local = pltpu.make_async_copy(key_hbm, key_ref, local_sem.at[3])
    key_local.start()
    embed = embed_ref[...].astype(F32)
    half = embed.shape[1] // 2
    folded = jnp.concatenate([embed[:, :half], embed[:, half:]], axis=0).astype(BF16)
    embed_own[...] = folded
    embed_all[me] = folded
    pl.semaphore_wait(barrier, pool)

    own_a, own_b = x * 2, x * 2 + 1
    other_a, other_b = 2 - x * 2, 3 - x * 2

    def own_weight(number):
        return weight_ref.at[pl.ds(pl.multiple_of(number * quarter, quarter), quarter)]

    b_piece, a_piece = weight_piece(own_b, me), weight_piece(own_a, me)
    send(enc_piece(me), to(near), source=enc_ref)
    send(enc_piece(me), to(mid), inner, source=enc_ref)
    send(enc_piece(me), to(side_y), source=enc_ref)
    send(b_piece, to(side_y), source=own_weight(own_b))
    send(embed_piece(me), to(near), source=embed_own)
    send(embed_piece(me), to(mid), inner, source=embed_own)
    send(embed_piece(me), to(side_y), source=embed_own)
    send(embed_piece(me), to(side_c), source=embed_own)
    send(enc_piece(me), to(side_c), source=enc_ref)
    send(b_piece, to(near), source=own_weight(own_b))
    send(b_piece, to(mid), inner, source=own_weight(own_b))
    send(a_piece, to(near), source=own_weight(own_a))
    send(a_piece, to(mid), inner, source=own_weight(own_a))
    send(a_piece, to(side_y), source=own_weight(own_a))
    for number in range(4):
        send(weight_piece(number, me), to(side_c), source=own_weight(number))

    def table_z(step):
        p = at(z_from[step], y, c)
        for piece in (enc_piece(p), embed_piece(p)):
            arrived(piece)
            send(piece, to(z_to[step]), inner)
            send(piece, to(side_y))
            send(piece, to(side_c))

    def table_y(step):
        p = at((z, *z_from)[step], 1 - y, c)
        for piece in (enc_piece(p), embed_piece(p)):
            arrived(piece)
            send(piece, to(side_c))

    def second_y():
        piece = weight_piece(own_b, side_y)
        arrived(piece)
        send(piece, to(near))
        send(piece, to(mid), inner)
        send(piece, X)
        send(piece, to(side_c))

    def second_z(step):
        for yy in (y, 1 - y):
            piece = weight_piece(own_b, at(z_from[step], yy, c))
            arrived(piece)
            send(piece, to(z_to[step]), inner)
            send(piece, X)
            send(piece, to(side_c))

    def first_z(step):
        piece = weight_piece(own_a, at(z_from[step], y, c))
        arrived(piece)
        send(piece, to(z_to[step]), inner)
        send(piece, to(side_y))
        send(piece, X)
        send(piece, to(side_c))

    def first_y(step):
        piece = weight_piece(own_a, at((z, *z_from)[step], 1 - y, c))
        arrived(piece)
        send(piece, X)
        send(piece, to(side_c))

    def over_x(number, zz, yy):
        piece = weight_piece(number, at(zz, yy, c))
        arrived(piece)
        send(piece, to(side_c))

    def over_x_z(step):
        for number, yy in ((other_b, y), (other_b, 1 - y), (other_a, y)):
            over_x(number, z_from[step], yy)

    def over_x_y(step):
        over_x(other_a, (z, *z_from)[step], 1 - y)

    tokens = enc_ref.shape[1]
    picks = owner_ref.shape[1]
    count = embed.shape[0]
    width = weight_ref.shape[1]
    head_dim = queries_ref.shape[1] // HEADS
    span = picks * tokens
    stretch = queries_ref.shape[0] // count
    scale = head_dim ** (-0.5)

    def scores():
        for zz in range(4):
            for yy in range(2):
                arrived(embed_piece(at(zz, yy, 1 - c)))
        key_local.wait()
        embeds = embed_all[...].reshape(-1, half)
        first = lax.dot_general(embeds, key_ref[:, :half], NT, preferred_element_type=F32)
        second = lax.dot_general(embeds, key_ref[:, half:], NT, preferred_element_type=F32)
        keys = first.shape[1]
        first = first.reshape(pool, 2 * count, keys)[:, :count]
        second = second.reshape(pool, 2 * count, keys)[:, count:]
        both = (first + second).reshape(pool * count, keys) * (2 * half) ** (-0.5)
        top = jnp.max(both, axis=1, keepdims=True)
        part = top + jnp.log(jnp.sum(jnp.exp(both - top), axis=1, keepdims=True))
        part_out[...] = jnp.broadcast_to(part, (pool * count, 128)).reshape(pool, count, 128)
        part_all[me] = part_out[me]
        for step in range(1, pool):
            d = (me + step) % pool
            copy = pltpu.make_async_remote_copy(
                src_ref=part_out.at[d], dst_ref=part_all.at[me], send_sem=send_sem.at[next(sites)],
                recv_sem=part_sem.at[me], device_id=to(d), device_id_type=MESH)
            copy.start()
            sends.append((copy, None))

    def pick():
        enc_local.wait()
        for zz in range(4):
            for yy in range(2):
                arrived(enc_piece(at(zz, yy, 1 - c)))
        for i in range(count):
            for t in range(picks):
                row = (i * picks + t) * tokens
                rows[row:row + tokens, :] = enc_all[owner_ref[i, t] * table + slot_ref[i, t]]

    def pair(zz, yy, cc):
        number = at(zz, yy, cc)
        lane = pl.multiple_of(number * width, width)
        pair_kv[0] = jnp.dot(rows[...], weight_all[number], preferred_element_type=F32).astype(BF16)
        pair_kv[1] = jnp.dot(
            rows[...], weight_all[number + pool // 2], preferred_element_type=F32).astype(BF16)
        zeros = jnp.zeros((stretch, head_dim), BF16)
        logits = []
        for i in range(count):
            q = queries_own[i * stretch:(i + 1) * stretch, pl.ds(lane, width)]
            q = jnp.concatenate([
                jnp.concatenate([q[:, :head_dim], zeros], axis=1),
                jnp.concatenate([zeros, q[:, head_dim:]], axis=1)], axis=0)
            logits.append(lax.dot_general(
                q, pair_kv[0, i * span:(i + 1) * span], NT, preferred_element_type=F32) * scale)
        probs = []
        for block in logits:
            expo = jnp.exp(block)
            probs.append((expo / jnp.sum(expo, axis=-1, keepdims=True)).astype(BF16))
        for i in range(count):
            mixed = jnp.dot(
                probs[i], pair_kv[1, i * span:(i + 1) * span], preferred_element_type=F32)
            mix_ref[i * stretch:(i + 1) * stretch, pl.ds(lane, width)] = jnp.concatenate(
                [mixed[:stretch, :head_dim], mixed[stretch:, head_dim:]], axis=1).astype(BF16)

    def other_core(zz):
        for yy in range(2):
            for source in (at(zz, yy, 1 - c), at(zz + 2, yy, 1 - c)):
                for number in range(4):
                    arrived(weight_piece(number, source))

    def pairs(zz, low):
        def body(step, carry):
            pair(zz, step % 2, (c + step // 2) % 2)
            return carry

        lax.fori_loop(low, low + 2, body, 0)

    near_z, far_z = z // 2, 1 - z // 2
    second_y()
    for step in range(3):
        table_z(step)
        first_z(step)
        second_z(step)
        table_y(step)
        first_y(step)
        if step == 0:
            over_x(other_b, z, 1 - y)
        else:
            over_x_z(step - 1)
            over_x_y(step - 1)
    table_y(3)
    scores()
    first_y(3)
    pick()
    weight_local.wait()
    queries_local.wait()
    over_x_y(2)
    pairs(near_z, 0)
    over_x_z(2)
    other_core(near_z)
    pairs(near_z, 2)
    over_x_y(3)
    pairs(far_z, 0)
    other_core(far_z)
    pairs(far_z, 2)
    for step in range(1, pool):
        p = (me + step) % pool
        pltpu.make_async_remote_copy(
            src_ref=part_out.at[0], dst_ref=part_all.at[p], send_sem=send_sem.at[0],
            recv_sem=part_sem.at[p], device_id=to(side_c), device_id_type=MESH).wait_recv()
    parts = part_all[...]
    largest = jnp.max(parts, axis=0)
    lse_ref[...] = largest + jnp.log(jnp.sum(jnp.exp(parts - largest[None]), axis=0))
    for copy, when in sends:
        if when is None:
            copy.wait_send()
        else:
            pl.when(when)(copy.wait_send)


def kernel_local(query_embed, key_slab, nbr_owner, nbr_slot, enc_table, stretch_queries, kv_weight):
    pool = lax.axis_size("pool")
    count, wide = query_embed.shape
    vmem = pl.BlockSpec(memory_space=pltpu.VMEM)
    smem = pl.BlockSpec(memory_space=pltpu.SMEM)
    hbm = pl.BlockSpec(memory_space=pltpu.HBM)
    dma = pltpu.SemaphoreType.DMA
    found = count * nbr_owner.shape[1] * enc_table.shape[1]
    lse, mix = pl.pallas_call(
        kernel,
        out_shape=(
            jax.ShapeDtypeStruct((count, 128), F32),
            jax.ShapeDtypeStruct(stretch_queries.shape, BF16),
        ),
        in_specs=[smem, smem, vmem, hbm, hbm, hbm, hbm],
        out_specs=(vmem, vmem),
        scratch_shapes=[
            pltpu.VMEM((pool * enc_table.shape[0],) + enc_table.shape[1:], BF16),
            pltpu.VMEM((pool,) + kv_weight.shape, BF16),
            pltpu.VMEM((2 * count, wide // 2), BF16),
            pltpu.VMEM((pool, 2 * count, wide // 2), BF16),
            pltpu.VMEM((pool, count, 128), F32),
            pltpu.VMEM((pool, count, 128), F32),
            pltpu.VMEM((found, enc_table.shape[2]), BF16),
            pltpu.VMEM(stretch_queries.shape, BF16),
            pltpu.VMEM((2, found, kv_weight.shape[1]), BF16),
            pltpu.VMEM(key_slab.shape, BF16),
            dma((130,)),
            dma((4,)),
            dma((pool,)),
            dma((pool,)),
            dma((pool * 4,)),
            dma((pool,)),
        ],
        compiler_params=pltpu.CompilerParams(
            collective_id=0, has_side_effects=True, vmem_limit_bytes=62 * 1024 * 1024),
    )(nbr_owner, nbr_slot, query_embed, key_slab, enc_table, stretch_queries, kv_weight)
    return lse[:, 0], mix


def gathered_local(query_embed, key_slab, nbr_owner, nbr_slot, enc_table, stretch_queries, kv_weight):
    me = lax.axis_index("pool")
    count = query_embed.shape[0]
    scores = lax.dot_general(
        lax.all_gather(query_embed, "pool", axis=0, tiled=True), key_slab, NT,
        preferred_element_type=F32) * query_embed.shape[1] ** (-0.5)
    top = jnp.max(scores, axis=1, keepdims=True)
    part = top[:, 0] + jnp.log(jnp.sum(jnp.exp(scores - top), axis=1))
    parts = lax.dynamic_slice_in_dim(lax.all_gather(part, "pool"), me * count, count, 1)
    largest = jnp.max(parts, axis=0)
    lse = largest + jnp.log(jnp.sum(jnp.exp(parts - largest), axis=0))
    table = lax.all_gather(enc_table, "pool", axis=0, tiled=True)
    wanted = (nbr_owner * enc_table.shape[0] + nbr_slot).reshape(-1)
    rows = jnp.concatenate(
        [lax.dynamic_index_in_dim(table, wanted[i], 0, False) for i in range(wanted.shape[0])], axis=0)
    projected = jnp.dot(
        rows, lax.all_gather(kv_weight, "pool", axis=1, tiled=True),
        preferred_element_type=F32).astype(BF16)
    width = stretch_queries.shape[1]
    head_dim = width // HEADS
    key_part = projected[:, :width].reshape(count, -1, HEADS, head_dim)
    value_part = projected[:, width:].reshape(count, -1, HEADS, head_dim)
    grouped = stretch_queries.reshape(count, -1, HEADS, head_dim)
    logits = jnp.einsum(
        "cqhd,ckhd->chqk", grouped, key_part, preferred_element_type=F32) * head_dim ** (-0.5)
    expo = jnp.exp(logits)
    probs = (expo / jnp.sum(expo, axis=-1, keepdims=True)).astype(BF16)
    mixed = jnp.einsum("chqk,ckhd->cqhd", probs, value_part, preferred_element_type=F32)
    return lse, mixed.astype(BF16).reshape(-1, width)


def solution(mesh):
    in_specs = (
        P(("groups", "pool"), None),
        P(("groups", "pool"), None),
        P(("groups", "pool"), None),
        P(("groups", "pool"), None),
        P(("groups", "pool"), None, None),
        P(("groups", "pool"), None),
        P(None, "pool"),
    )
    out_specs = (P(("groups", "pool")), P(("groups", "pool"), None))
    routed = mesh.shape["groups"] == 2 and mesh.shape["pool"] == 16
    return jax.shard_map(
        kernel_local if routed else gathered_local, mesh=mesh, in_specs=in_specs, out_specs=out_specs,
        check_vma=False)
```

```python
import functools

import jax
import jax.numpy as jnp
from jax import lax
from jax.experimental import pallas as pl
from jax.experimental.pallas import tpu as pltpu
from jax.sharding import PartitionSpec as P

HEADS = 16
MESH = pl.DeviceIdType.MESH
F32 = jnp.float32
BF16 = jnp.bfloat16
NT = (((1,), (1,)), ((), ()))


def kernel(
    owner_ref, slot_ref, embed_ref, key_hbm, enc_ref, queries_ref, weight_ref,
    lse_ref, mix_ref,
    enc_all, weight_all, embed_own, embed_all, part_out, part_all, rows, queries_own, pair_kv, key_ref,
    send_sem, local_sem, enc_sem, embed_sem, weight_sem, part_sem,
):
    pool = lax.axis_size("pool")
    x = lax.axis_index("groups")
    me = lax.axis_index("pool")
    z, y, c = me // 4, (me // 2) % 2, me % 2
    table = enc_ref.shape[0]
    quarter = weight_ref.shape[0] // 4
    sites = iter(range(send_sem.shape[0]))
    sends = []
    inner = (z + 1) // 2 == 1

    def at(zz, yy, cc):
        return (zz * 2 + yy) * 2 + cc

    side_y, side_c = at(z, 1 - y, c), at(z, y, 1 - c)
    near, mid = at(z + 1 - 2 * (z % 2), y, c), at(3 - z, y, c)
    z_from = (z + 1 - 2 * (z % 2), 2 - z // 2, 3 - 3 * (z // 2))
    z_to = (at(3 - z, y, c), at(3 * z - 3, y, c), at(3 * z - 3, y, c))
    X = {"groups": 1 - x, "pool": me}

    def to(pool_index):
        return {"groups": x, "pool": pool_index}

    def enc_piece(p, entry):
        return enc_all.at[p * table + entry], enc_sem.at[p * table + entry]

    def embed_piece(p):
        return embed_all.at[p], embed_sem.at[p]

    def weight_piece(number, p):
        start = pl.multiple_of(number * quarter, quarter)
        return weight_all.at[p, pl.ds(start, quarter)], weight_sem.at[p * 4 + number]

    def send(piece, target, when=None, source=None):
        ref, sem = piece
        index = next(sites)
        copy = pltpu.make_async_remote_copy(
            src_ref=ref if source is None else source, dst_ref=ref, send_sem=send_sem.at[index],
            recv_sem=sem, device_id=target, device_id_type=MESH)
        sends.append((copy, when))
        if when is None:
            copy.start()
        else:
            pl.when(when)(copy.start)

    def arrived(piece):
        ref, sem = piece
        pltpu.make_async_remote_copy(
            src_ref=ref, dst_ref=ref, send_sem=send_sem.at[0], recv_sem=sem, device_id=to(side_c),
            device_id_type=MESH).wait_recv()

    barrier = pltpu.get_barrier_semaphore()
    for step in range(1, pool):
        pl.semaphore_signal(barrier, inc=1, device_id=to((me + step) % pool), device_id_type=MESH)
    pl.semaphore_signal(barrier, inc=1, device_id=X, device_id_type=MESH)

    enc_local = pltpu.make_async_copy(enc_ref, enc_all.at[pl.ds(me * table, table)], local_sem.at[0])
    enc_local.start()
    weight_local = pltpu.make_async_copy(weight_ref, weight_all.at[me], local_sem.at[1])
    weight_local.start()
    queries_local = pltpu.make_async_copy(queries_ref, queries_own, local_sem.at[2])
    queries_local.start()
    key_local = pltpu.make_async_copy(key_hbm, key_ref, local_sem.at[3])
    key_local.start()
    embed = embed_ref[...].astype(F32)
    half = embed.shape[1] // 2
    folded = jnp.concatenate([embed[:, :half], embed[:, half:]], axis=0).astype(BF16)
    embed_own[...] = folded
    embed_all[me] = folded
    pl.semaphore_wait(barrier, pool)

    own_a, own_b = x * 2, x * 2 + 1
    other_a, other_b = 2 - x * 2, 3 - x * 2

    def own_weight(number):
        return weight_ref.at[pl.ds(pl.multiple_of(number * quarter, quarter), quarter)]

    b_piece, a_piece = weight_piece(own_b, me), weight_piece(own_a, me)
    def own_table(entry):
        piece, source = enc_piece(me, entry), enc_ref.at[entry]
        send(piece, to(near), source=source)
        send(piece, to(mid), inner, source=source)
        send(piece, to(side_y), source=source)
        send(piece, to(side_c), source=source)

    send(b_piece, to(side_y), source=own_weight(own_b))
    own_table(0)
    send(embed_piece(me), to(near), source=embed_own)
    send(embed_piece(me), to(mid), inner, source=embed_own)
    send(embed_piece(me), to(side_y), source=embed_own)
    send(embed_piece(me), to(side_c), source=embed_own)
    own_table(1)
    send(a_piece, to(near), source=own_weight(own_a))
    send(a_piece, to(mid), inner, source=own_weight(own_a))
    send(a_piece, to(side_y), source=own_weight(own_a))
    own_table(2)
    send(b_piece, to(near), source=own_weight(own_b))
    send(b_piece, to(mid), inner, source=own_weight(own_b))
    own_table(3)
    for number in range(4):
        send(weight_piece(number, me), to(side_c), source=own_weight(number))

    def hand_z(piece, step):
        arrived(piece)
        send(piece, to(z_to[step]), inner)
        send(piece, to(side_y))
        send(piece, to(side_c))

    def hand_y(piece):
        arrived(piece)
        send(piece, to(side_c))

    def table_z(step, entry):
        hand_z(enc_piece(at(z_from[step], y, c), entry), step)

    def table_y(step, entry):
        hand_y(enc_piece(at((z, *z_from)[step], 1 - y, c), entry))

    def embed_z(step):
        hand_z(embed_piece(at(z_from[step], y, c)), step)

    def embed_y(step):
        hand_y(embed_piece(at((z, *z_from)[step], 1 - y, c)))

    def second_y():
        piece = weight_piece(own_b, side_y)
        arrived(piece)
        send(piece, to(near))
        send(piece, to(mid), inner)
        send(piece, X)
        send(piece, to(side_c))

    def second_z(step, yy):
        piece = weight_piece(own_b, at(z_from[step], yy, c))
        arrived(piece)
        send(piece, to(z_to[step]), inner)
        send(piece, X)
        send(piece, to(side_c))

    def first_z(step):
        piece = weight_piece(own_a, at(z_from[step], y, c))
        arrived(piece)
        send(piece, to(z_to[step]), inner)
        send(piece, to(side_y))
        send(piece, X)
        send(piece, to(side_c))

    def first_y(step):
        piece = weight_piece(own_a, at((z, *z_from)[step], 1 - y, c))
        arrived(piece)
        send(piece, X)
        send(piece, to(side_c))

    def over_x(number, zz, yy):
        piece = weight_piece(number, at(zz, yy, c))
        arrived(piece)
        send(piece, to(side_c))

    def over_x_z(step):
        for number, yy in ((other_b, y), (other_b, 1 - y), (other_a, y)):
            over_x(number, z_from[step], yy)

    def over_x_y(step):
        over_x(other_a, (z, *z_from)[step], 1 - y)

    tokens = enc_ref.shape[1]
    picks = owner_ref.shape[0]
    count = embed.shape[0]
    width = weight_ref.shape[1]
    head_dim = queries_ref.shape[1] // HEADS
    span = picks * tokens
    stretch = queries_ref.shape[0] // count
    scale = head_dim ** (-0.5)

    def scores():
        for zz in range(4):
            for yy in range(2):
                arrived(embed_piece(at(zz, yy, 1 - c)))
        key_local.wait()
        embeds = embed_all[...].reshape(-1, half)
        first = lax.dot_general(embeds, key_ref[:, :half], NT, preferred_element_type=F32)
        second = lax.dot_general(embeds, key_ref[:, half:], NT, preferred_element_type=F32)
        keys = first.shape[1]
        first = first.reshape(pool, 2 * count, keys)[:, :count]
        second = second.reshape(pool, 2 * count, keys)[:, count:]
        both = (first + second).reshape(pool * count, keys) * (2 * half) ** (-0.5)
        top = jnp.max(both, axis=1, keepdims=True)
        part = top + jnp.log(jnp.sum(jnp.exp(both - top), axis=1, keepdims=True))
        part_out[...] = jnp.broadcast_to(part, (pool * count, 128)).reshape(pool, count, 128)
        part_all[me] = part_out[me]
        for step in range(1, pool):
            d = (me + step) % pool
            copy = pltpu.make_async_remote_copy(
                src_ref=part_out.at[d], dst_ref=part_all.at[me], send_sem=send_sem.at[next(sites)],
                recv_sem=part_sem.at[me], device_id=to(d), device_id_type=MESH)
            copy.start()
            sends.append((copy, None))

    def pick():
        enc_local.wait()
        for zz in range(4):
            for yy in range(2):
                for entry in range(table):
                    arrived(enc_piece(at(zz, yy, 1 - c), entry))
        for i in range(count):
            for t in range(picks):
                row = (i * picks + t) * tokens
                rows[row:row + tokens, :] = enc_all[owner_ref[t, i] * table + slot_ref[t, i]]

    def pair(zz, yy, cc):
        number = at(zz, yy, cc)
        lane = pl.multiple_of(number * width, width)
        pair_kv[0] = jnp.dot(rows[...], weight_all[number], preferred_element_type=F32).astype(BF16)
        pair_kv[1] = jnp.dot(
            rows[...], weight_all[number + pool // 2], preferred_element_type=F32).astype(BF16)
        zeros = jnp.zeros((stretch, head_dim), BF16)
        logits = []
        for i in range(count):
            q = queries_own[i * stretch:(i + 1) * stretch, pl.ds(lane, width)]
            q = jnp.concatenate([
                jnp.concatenate([q[:, :head_dim], zeros], axis=1),
                jnp.concatenate([zeros, q[:, head_dim:]], axis=1)], axis=0)
            logits.append(lax.dot_general(
                q, pair_kv[0, i * span:(i + 1) * span], NT, preferred_element_type=F32) * scale)
        probs = []
        for block in logits:
            expo = jnp.exp(block)
            probs.append((expo / jnp.sum(expo, axis=-1, keepdims=True)).astype(BF16))
        for i in range(count):
            mixed = jnp.dot(
                probs[i], pair_kv[1, i * span:(i + 1) * span], preferred_element_type=F32)
            mix_ref[i * stretch:(i + 1) * stretch, pl.ds(lane, width)] = jnp.concatenate(
                [mixed[:stretch, :head_dim], mixed[stretch:, head_dim:]], axis=1).astype(BF16)

    def other_core(zz):
        for yy in range(2):
            for source in (at(zz, yy, 1 - c), at(zz + 2, yy, 1 - c)):
                for number in range(4):
                    arrived(weight_piece(number, source))

    def pairs(zz, low):
        def body(step, carry):
            pair(zz, step % 2, (c + step // 2) % 2)
            return carry

        lax.fori_loop(low, low + 2, body, 0)

    near_z, far_z = z // 2, 1 - z // 2
    second_y()
    for step in range(3):
        table_z(step, 0)
        embed_z(step)
        table_y(step, 0)
        embed_y(step)
        table_z(step, 1)
        table_y(step, 1)
        first_z(step)
        table_z(step, 2)
        first_y(step)
        table_y(step, 2)
        second_z(step, y)
        table_z(step, 3)
        second_z(step, 1 - y)
        table_y(step, 3)
        if step == 0:
            over_x(other_b, z, 1 - y)
        else:
            over_x_z(step - 1)
            over_x_y(step - 1)
    embed_y(3)
    for entry in range(table):
        table_y(3, entry)
    scores()
    first_y(3)
    pick()
    weight_local.wait()
    queries_local.wait()
    over_x_y(2)
    pairs(near_z, 0)
    over_x_z(2)
    other_core(near_z)
    pairs(near_z, 2)
    over_x_y(3)
    pairs(far_z, 0)
    other_core(far_z)
    pairs(far_z, 2)
    for step in range(1, pool):
        p = (me + step) % pool
        pltpu.make_async_remote_copy(
            src_ref=part_out.at[0], dst_ref=part_all.at[p], send_sem=send_sem.at[0],
            recv_sem=part_sem.at[p], device_id=to(side_c), device_id_type=MESH).wait_recv()
    parts = part_all[...]
    largest = jnp.max(parts, axis=0)
    lse_ref[...] = largest + jnp.log(jnp.sum(jnp.exp(parts - largest[None]), axis=0))
    for copy, when in sends:
        if when is None:
            copy.wait_send()
        else:
            pl.when(when)(copy.wait_send)


def kernel_local(query_embed, key_slab, nbr_owner, nbr_slot, enc_table, stretch_queries, kv_weight):
    pool = lax.axis_size("pool")
    count, wide = query_embed.shape
    vmem = pl.BlockSpec(memory_space=pltpu.VMEM)
    smem = pl.BlockSpec(memory_space=pltpu.SMEM)
    hbm = pl.BlockSpec(memory_space=pltpu.HBM)
    dma = pltpu.SemaphoreType.DMA
    found = count * nbr_owner.shape[1] * enc_table.shape[1]
    lse, mix = pl.pallas_call(
        kernel,
        out_shape=(
            jax.ShapeDtypeStruct((count, 128), F32),
            jax.ShapeDtypeStruct(stretch_queries.shape, BF16),
        ),
        in_specs=[smem, smem, vmem, hbm, hbm, hbm, hbm],
        out_specs=(vmem, vmem),
        scratch_shapes=[
            pltpu.VMEM((pool * enc_table.shape[0],) + enc_table.shape[1:], BF16),
            pltpu.VMEM((pool,) + kv_weight.shape, BF16),
            pltpu.VMEM((2 * count, wide // 2), BF16),
            pltpu.VMEM((pool, 2 * count, wide // 2), BF16),
            pltpu.VMEM((pool, count, 128), F32),
            pltpu.VMEM((pool, count, 128), F32),
            pltpu.VMEM((found, enc_table.shape[2]), BF16),
            pltpu.VMEM(stretch_queries.shape, BF16),
            pltpu.VMEM((2, found, kv_weight.shape[1]), BF16),
            pltpu.VMEM(key_slab.shape, BF16),
            dma((190,)),
            dma((4,)),
            dma((pool * enc_table.shape[0],)),
            dma((pool,)),
            dma((pool * 4,)),
            dma((pool,)),
        ],
        compiler_params=pltpu.CompilerParams(
            collective_id=0, has_side_effects=True, vmem_limit_bytes=62 * 1024 * 1024),
    )(nbr_owner.T, nbr_slot.T, query_embed, key_slab, enc_table, stretch_queries, kv_weight)
    return lse[:, 0], mix


def gathered_local(query_embed, key_slab, nbr_owner, nbr_slot, enc_table, stretch_queries, kv_weight):
    me = lax.axis_index("pool")
    count = query_embed.shape[0]
    scores = lax.dot_general(
        lax.all_gather(query_embed, "pool", axis=0, tiled=True), key_slab, NT,
        preferred_element_type=F32) * query_embed.shape[1] ** (-0.5)
    top = jnp.max(scores, axis=1, keepdims=True)
    part = top[:, 0] + jnp.log(jnp.sum(jnp.exp(scores - top), axis=1))
    parts = lax.dynamic_slice_in_dim(lax.all_gather(part, "pool"), me * count, count, 1)
    largest = jnp.max(parts, axis=0)
    lse = largest + jnp.log(jnp.sum(jnp.exp(parts - largest), axis=0))
    table = lax.all_gather(enc_table, "pool", axis=0, tiled=True)
    wanted = (nbr_owner * enc_table.shape[0] + nbr_slot).reshape(-1)
    rows = jnp.concatenate(
        [lax.dynamic_index_in_dim(table, wanted[i], 0, False) for i in range(wanted.shape[0])], axis=0)
    projected = jnp.dot(
        rows, lax.all_gather(kv_weight, "pool", axis=1, tiled=True),
        preferred_element_type=F32).astype(BF16)
    width = stretch_queries.shape[1]
    head_dim = width // HEADS
    key_part = projected[:, :width].reshape(count, -1, HEADS, head_dim)
    value_part = projected[:, width:].reshape(count, -1, HEADS, head_dim)
    grouped = stretch_queries.reshape(count, -1, HEADS, head_dim)
    logits = jnp.einsum(
        "cqhd,ckhd->chqk", grouped, key_part, preferred_element_type=F32) * head_dim ** (-0.5)
    expo = jnp.exp(logits)
    probs = (expo / jnp.sum(expo, axis=-1, keepdims=True)).astype(BF16)
    mixed = jnp.einsum("chqk,ckhd->cqhd", probs, value_part, preferred_element_type=F32)
    return lse, mixed.astype(BF16).reshape(-1, width)


def solution(mesh):
    in_specs = (
        P(("groups", "pool"), None),
        P(("groups", "pool"), None),
        P(("groups", "pool"), None),
        P(("groups", "pool"), None),
        P(("groups", "pool"), None, None),
        P(("groups", "pool"), None),
        P(None, "pool"),
    )
    out_specs = (P(("groups", "pool")), P(("groups", "pool"), None))
    routed = mesh.shape["groups"] == 2 and mesh.shape["pool"] == 16
    return jax.shard_map(
        kernel_local if routed else gathered_local, mesh=mesh, in_specs=in_specs, out_specs=out_specs,
        check_vma=False)
```
